32 devices in a mesh: dp: 4 (over y, core), tile: 8 (over z, x).
Axes of the slice: x: 2, y: 2, z: 4, core: 2. Of those that a mesh axis runs over, the one named last changes fastest.
Arguments:
- video_in: bfloat16 [4, 16, 32, 8, 256], P('dp', None, 'tile'), may hold values from -12 to 12
- clip_lengths: int32 [4, 6], P('dp'), may hold values from 1 to 5, 16 in all within a row
- norm_gain: float32 [256], replicated, may hold values from 0.1 to 1.9
- norm_bias: float32 [256], replicated, may hold values from -3 to 3
- spatial_weight: bfloat16 [3, 3, 256, 256], replicated, may hold values from -0.125 to 0.125
- temporal_weight: bfloat16 [3, 256, 256], replicated, may hold values from -0.21875 to 0.21875
- cotangent: bfloat16 [4, 16, 32, 8, 256], P('dp', 'tile'), may hold values from -6 to 6
Outputs:
- encoded: bfloat16 [4, 16, 32, 8, 256], P('dp', 'tile')
- spatial_grad: float32 [3, 3, 256, 256], replicated
- temporal_grad: float32 [3, 256, 256], replicated
The draws below stay inside these ranges and needn't reach their ends.
Inputs may be any that keep to these rules, and one draw needn't show every extreme that they name: `clip_lengths`: the lengths of each batch sum to 16.
All inputs are finite; a program needn't handle non-finite values.
Results may differ from the reference program's by a relative error of at most 0.005.
Values may be sent and summed in bfloat16 or wider, within the bound.
A program may use at most 64 MiB of HBM per device.

```python
import math
import jax
import jax.numpy as jnp
import numpy as np
from jax import lax

C = 256
GROUPS = 32
NCLIP = 6
W = 8
BATCHES = 4
FRAMES = 16
H = 32


def draw_video_in(key, part):
    noise_key, chan_key = jax.random.split(key, 2)
    row_scale = jnp.exp(jnp.log(3.0) * jnp.arange(H, dtype=jnp.float32) / (H - 1))
    chan_scale = jnp.exp(jax.random.uniform(chan_key, (C,), jnp.float32, jnp.log(0.3), jnp.log(3.0)))
    full_shape = (BATCHES, FRAMES, H, W, C)
    noise_vals = jax.random.normal(noise_key, full_shape, jnp.float32)
    values = noise_vals * row_scale[None, None, :, None, None] * chan_scale
    return jnp.clip(values, -12.0, 12.0).astype(jnp.bfloat16)


def block_levels(rng, shape, cuts, smallest, top_value):
    gain, own = 1.0, jax.random.fold_in(rng, 6)
    for axis_at, parts in cuts:
        steps = jnp.exp(jax.random.uniform(jax.random.fold_in(own, axis_at), (parts,), jnp.float32, smallest / len(cuts), top_value / len(cuts)))
        gain = gain * jnp.repeat(steps, shape[axis_at] // parts).reshape([-1 if axis == axis_at else 1 for axis in range(len(shape))])
    return gain


def length_profile(count, total, most, slope):
    loads = [(1 << 20) // math.isqrt(standing ** slope) + 1 for standing in range(2, count + 1)]
    surplus, holding = total - most - (count - 1), [1] * (count - 1)
    while surplus > 0:
        candidates = [i for i in range(count - 1) if holding[i] < most]
        mass, remaining = sum([loads[i] for i in candidates]), surplus
        for i in candidates:
            addition = min(most - holding[i], max(1, remaining * loads[i] // mass), surplus)
            holding[i] = holding[i] + addition
            surplus = surplus - addition
    return np.array([most] + holding)


def ragged_sizes(rng, count, total, limit, lean):
    if count == 2:
        one = jax.random.randint(rng, (), max(1, total - limit), min(limit, total - 1) + 1)
        return jnp.stack([one, total - one])
    sizes = jnp.asarray(length_profile(count, total, limit, lean), jnp.int32)
    twos = (count - 1) // 2
    giver, receiver = sizes[1:1 + 2 * twos:2], sizes[2:2 + 2 * twos:2]
    room = jnp.minimum(giver - 1, limit - receiver)
    passed = jax.random.randint(jax.random.fold_in(rng, 1), (twos,), 0, 1 << 20) % (room + 1)
    sizes = sizes.at[1:1 + 2 * twos:2].set(giver - passed).at[2:2 + 2 * twos:2].set(receiver + passed)
    return sizes[jax.random.permutation(jax.random.fold_in(rng, 2), count)]


def normal_values(key, dims, width, bound, cuts=(), kind=jnp.bfloat16):
    result = jax.random.normal(key, dims, jnp.float32) * width
    if len(cuts) > 0:
        result = block_levels(key, dims, cuts, -0.22, 0.18) * result
    return jnp.clip(result, min=-bound, max=bound).astype(kind)


def setup_inputs(seed: int = 0) -> dict:
    seeds = jax.random.split(jax.random.key(seed), 8)
    return {
        "video_in": draw_video_in(jax.random.fold_in(seeds[7], 71), 0),
        "clip_lengths": jax.vmap(lambda own: ragged_sizes(own, NCLIP, FRAMES, FRAMES // 3, 2))(jax.random.split(seeds[1], BATCHES)).reshape((BATCHES, NCLIP)).astype(jnp.int32),
        "norm_gain": jnp.clip(1.0 + 0.18 * jax.random.normal(seeds[2], (C,), jnp.float32), 0.1, 1.9),
        "norm_bias": normal_values(seeds[3], (C,), 0.5, 3.0, (), jnp.float32),
        "spatial_weight": normal_values(seeds[4], (3, 3, C, C), (9 * C) ** -0.5, 0.125),
        "temporal_weight": normal_values(seeds[5], (3, C, C), (3 * C) ** -0.5, 0.21875),
        "cotangent": normal_values(seeds[6], (BATCHES, FRAMES, H, W, C), 1.0, 6.0, ((0, 4), (1, 8))),
    }


norm_eps = 1e-05

def clip_tables(lengths, frame_total):
    clip_ends = jnp.cumsum(lengths).astype(jnp.int32)
    clip_starts = (clip_ends - lengths).astype(jnp.int32)
    frame_ids = jnp.arange(frame_total, dtype=jnp.int32)
    membership = (frame_ids[:, None] >= clip_starts[None, :]) & (frame_ids[:, None] < clip_ends[None, :])
    clip_first = lax.optimization_barrier(jnp.sum(jnp.where(membership, clip_starts[None, :], 0), axis=1)).astype(jnp.int32)
    return (membership.astype(jnp.float32), (frame_ids - clip_first).astype(jnp.int32))

def group_total(onehot, frame_term, group_count):
    clip_term = jnp.dot(onehot.T, frame_term, precision=lax.Precision.HIGHEST)
    return clip_term.reshape(clip_term.shape[0], group_count, -1).sum(axis=2)

def spread_back(onehot, clip_group, channels):
    per_channel = jnp.repeat(clip_group, channels // clip_group.shape[1], axis=1)
    return jnp.dot(onehot, per_channel, precision=lax.Precision.HIGHEST)

def patch_columns(padded, strip_rows, frame_width):
    pieces = [padded[:, row_step:row_step + strip_rows, col_step:col_step + frame_width, :] for row_step in range(3) for col_step in range(3)]
    return jnp.concatenate(pieces, axis=-1).reshape(-1, 9 * padded.shape[-1])

def earlier_stack(block_ext, pos_here):
    frame_count = pos_here.shape[0]
    stacked = []
    for offset in range(3):
        keep = (pos_here >= offset)[:, None, None, None]
        window = block_ext[2 - offset:2 - offset + frame_count]
        stacked.append(jnp.where(keep, window, jnp.zeros_like(window)))
    return jnp.concatenate(stacked, axis=-1)

def later_stack(cot_ext, pos_ahead):
    frame_count = pos_ahead.shape[0] - 2
    stacked = []
    for offset in range(3):
        keep = (pos_ahead[offset:offset + frame_count] >= offset)[:, None, None, None]
        window = cot_ext[offset:offset + frame_count]
        stacked.append(jnp.where(keep, window, jnp.zeros_like(window)))
    return jnp.concatenate(stacked, axis=-1)

def temporal_pass(block_ext, cot_ext, pos_here, pos_ahead, temporal_weight):
    channels = temporal_weight.shape[1]
    frame_count = pos_here.shape[0]
    earlier = earlier_stack(block_ext, pos_here).reshape(-1, 3 * channels)
    block_now = block_ext[2:]
    lifted = jnp.dot(earlier, temporal_weight.reshape(3 * channels, channels), preferred_element_type=jnp.float32)
    encoded = (block_now.astype(jnp.float32) + lifted.reshape(block_now.shape)).astype(jnp.bfloat16)
    cot_now = cot_ext[:frame_count]
    later_cot = later_stack(cot_ext, pos_ahead).reshape(-1, 3 * channels)
    back_weight = jnp.transpose(temporal_weight, (0, 2, 1)).reshape(3 * channels, channels)
    pulled = jnp.dot(later_cot, back_weight, preferred_element_type=jnp.float32)
    grad_block = (cot_now.astype(jnp.float32) + pulled.reshape(cot_now.shape)).astype(jnp.bfloat16)
    temporal_term = jnp.dot(earlier.T, cot_now.reshape(-1, channels), preferred_element_type=jnp.float32)
    return (encoded, grad_block, temporal_term)

def reference(video_in, clip_lengths, norm_gain, norm_bias, spatial_weight, temporal_weight, cotangent):
    channels = video_in.shape[4]
    spatial_flat = spatial_weight.reshape(9 * channels, channels)

    def one_batch(items):
        video_one, lengths, cot_one = items
        frame_total, height, frame_width = (video_one.shape[0], video_one.shape[1], video_one.shape[2])
        onehot, position = clip_tables(lengths, frame_total)
        local_vals = video_one.astype(jnp.float32)
        per_group = channels // GROUPS
        counts = lengths.astype(jnp.float32) * (height * frame_width * per_group)
        clip_mean = group_total(onehot, lax.optimization_barrier(jnp.sum(local_vals, axis=(1, 2))), GROUPS) / counts[:, None]
        centered = local_vals - spread_back(onehot, clip_mean, channels)[:, None, None, :]
        clip_var = group_total(onehot, lax.optimization_barrier(jnp.sum(centered * centered, axis=(1, 2))), GROUPS) / counts[:, None]
        rstd_frame = spread_back(onehot, lax.rsqrt(clip_var + norm_eps), channels)
        normed = centered * rstd_frame[:, None, None, :] * norm_gain + norm_bias
        active = jax.nn.silu(normed).astype(jnp.bfloat16)
        padded = jnp.pad(active, ((0, 0), (1, 1), (1, 1), (0, 0)))
        columns = patch_columns(padded, height, frame_width)
        conv_out = jnp.dot(columns, spatial_flat, preferred_element_type=jnp.float32)
        block_out = (local_vals + conv_out.reshape(local_vals.shape)).astype(jnp.bfloat16)
        blank_frames = jnp.zeros((2, height, frame_width, channels), jnp.bfloat16)
        block_ext = jnp.concatenate([blank_frames, block_out], axis=0)
        cot_ext = jnp.concatenate([cot_one, blank_frames], axis=0)
        pos_ahead = jnp.concatenate([position, jnp.zeros((2,), jnp.int32)], axis=0)
        encoded, grad_block, temporal_term = temporal_pass(block_ext, cot_ext, position, pos_ahead, temporal_weight)
        spatial_term = jnp.dot(columns.T, grad_block.reshape(-1, channels), preferred_element_type=jnp.float32)
        return (encoded, spatial_term, temporal_term)
    encoded, spatial_terms, temporal_terms = lax.map(one_batch, (video_in, clip_lengths, cotangent))
    pixel_total = video_in.shape[0] * video_in.shape[1] * video_in.shape[2] * video_in.shape[3]
    grad_scale = 1.0 / math.sqrt(pixel_total)
    spatial_grad = (lax.optimization_barrier(jnp.sum(spatial_terms, axis=0)) * grad_scale).reshape(3, 3, channels, channels)
    temporal_grad = (lax.optimization_barrier(jnp.sum(temporal_terms, axis=0)) * grad_scale).reshape(3, channels, channels)
    return (encoded, spatial_grad, temporal_grad)
```

```python
import functools
import math

import jax
import jax.numpy as jnp
from jax import lax
from jax.experimental import pallas as pl
from jax.experimental.pallas import tpu as pltpu
from jax.sharding import PartitionSpec as P

GROUPS = 32
MESH = pl.DeviceIdType.MESH
norm_eps = 1e-05


def remote(src, dst, send, recv, peer):
    return pltpu.make_async_remote_copy(
        src_ref=src,
        dst_ref=dst,
        send_sem=send,
        recv_sem=recv,
        device_id=peer,
        device_id_type=MESH,
    )


def exchange_kernel(
    tiles,
    video_ref,
    top_ref,
    bot_ref,
    cot_ref,
    stats_ref,
    rows_ref,
    above_ref,
    below_ref,
    mine,
    theirs,
    stat_send,
    stat_recv,
    halo_send,
    halo_recv,
    cot_send,
    cot_recv,
):
    dp, me = lax.axis_index("dp"), lax.axis_index("tile")
    frames, cells, channels = video_ref.shape
    frame_dev = cot_ref.shape[0]
    barrier = pltpu.get_barrier_semaphore()
    peers = [lax.rem(me + k, tiles) for k in range(1, tiles)]
    for peer in peers:
        pl.semaphore_signal(barrier, inc=1, device_id=(dp, peer), device_id_type=MESH)
    values = video_ref[...].astype(jnp.float32)
    sums = jnp.concatenate(
        [jnp.sum(values, axis=1), jnp.sum(values * values, axis=1)], axis=0
    )
    lanes = mine.shape[1]
    per_group = channels // GROUPS
    member = lax.broadcasted_iota(jnp.int32, (channels, lanes), 0) // per_group
    group = lax.broadcasted_iota(jnp.int32, (channels, lanes), 1)
    pick = jnp.where(member == group, 1.0, 0.0).astype(jnp.float32)
    mine[...] = jnp.dot(
        sums, pick, precision=lax.Precision.HIGHEST, preferred_element_type=jnp.float32
    )
    pl.semaphore_wait(barrier, tiles - 1)
    stats = []
    for k, peer in enumerate(peers):
        copy = remote(mine, theirs.at[k], stat_send.at[k], stat_recv.at[k], (dp, peer))
        copy.start()
        stats.append(copy)
    up = remote(top_ref, below_ref, halo_send.at[0], halo_recv.at[0], (dp, me - 1))
    down = remote(bot_ref, above_ref, halo_send.at[1], halo_recv.at[1], (dp, me + 1))

    @pl.when(me > 0)
    def _():
        up.start()

    @pl.when(me < tiles - 1)
    def _():
        down.start()

    moves = []
    for k, peer in enumerate(peers):
        copy = remote(
            cot_ref.at[:, pl.ds(peer * cells, cells)],
            rows_ref.at[pl.ds(me * frame_dev, frame_dev)],
            cot_send.at[k],
            cot_recv.at[k],
            (dp, peer),
        )
        copy.start()
        moves.append(copy)
    rows_ref[pl.ds(me * frame_dev, frame_dev)] = cot_ref[:, pl.ds(me * cells, cells)]
    total = mine[...]
    for k, copy in enumerate(stats):
        copy.wait_recv()
        total = total + theirs[k]
    stats_ref[...] = total

    @pl.when(me > 0)
    def _():
        up.wait_send()
        down.wait_recv()

    @pl.when(me < tiles - 1)
    def _():
        down.wait_send()
        up.wait_recv()

    for copy in stats:
        copy.wait_send()
    for copy in moves:
        copy.wait()


def exchange(video, top, bot, cot, tiles):
    frames, cells, channels = video.shape
    vmem = pl.BlockSpec(memory_space=pltpu.VMEM)
    dma = pltpu.SemaphoreType.DMA
    return pl.pallas_call(
        functools.partial(exchange_kernel, tiles),
        out_shape=[
            jax.ShapeDtypeStruct((2 * frames, 128), jnp.float32),
            jax.ShapeDtypeStruct((frames, cells, channels), jnp.bfloat16),
            jax.ShapeDtypeStruct(top.shape, jnp.bfloat16),
            jax.ShapeDtypeStruct(top.shape, jnp.bfloat16),
        ],
        in_specs=[vmem] * 4,
        out_specs=[vmem] * 4,
        scratch_shapes=[
            pltpu.VMEM((2 * frames, 128), jnp.float32),
            pltpu.VMEM((tiles - 1, 2 * frames, 128), jnp.float32),
            dma((tiles - 1,)),
            dma((tiles - 1,)),
            dma((2,)),
            dma((2,)),
            dma((tiles - 1,)),
            dma((tiles - 1,)),
        ],
        compiler_params=pltpu.CompilerParams(
            collective_id=0, has_side_effects=True, vmem_limit_bytes=32 << 20
        ),
    )(video, top, bot, cot)


def digits(dps, tiles):
    dp, tile = lax.axis_index("dp"), lax.axis_index("tile")
    return {
        "core": (2, lax.rem(dp, 2), lambda j: ((dp // 2) * 2 + j, tile)),
        "y": (dps // 2, dp // 2, lambda j: (j * 2 + lax.rem(dp, 2), tile)),
        "lo": (2, lax.rem(tile, 2), lambda j: (dp, (tile // 2) * 2 + j)),
        "hi": (tiles // 2, tile // 2, lambda j: (dp, j * 2 + lax.rem(tile, 2))),
    }


ORDERS = (("core", "lo", "y", "hi"), ("core", "y", "lo", "hi"))


def group_sizes(order, dps, tiles):
    known = {"core": 2, "y": dps // 2, "lo": 2, "hi": tiles // 2}
    return [known[name] for name in order]


def reduce_kernel(dps, tiles, enc_ref, grad_ref, out_ref, sum_ref, *scratch):
    chunks, pieces = grad_ref.shape[:2]
    scratch = list(scratch)
    enc_send, enc_recv, sends, recvs = scratch[-4:]
    bufs = scratch[:-4]
    dp, me = lax.axis_index("dp"), lax.axis_index("tile")
    frames, cells, _ = enc_ref.shape
    frame_dev = out_ref.shape[0]
    table = digits(dps, tiles)
    peers = [(dp, lax.rem(me + k, tiles)) for k in range(1, tiles)]
    greet = list(peers)
    for name in ("core", "y"):
        size, mine, peer = table[name]
        greet += [peer(lax.rem(mine + k, size)) for k in range(1, size)]
    barrier = pltpu.get_barrier_semaphore()
    for peer in greet:
        pl.semaphore_signal(barrier, inc=1, device_id=peer, device_id_type=MESH)
    pl.semaphore_wait(barrier, len(greet))

    used = [0]
    waiting = []

    def send(src, dst, peer):
        at = used[0]
        used[0] += 1
        copy = remote(src, dst, sends.at[at], recvs.at[at], peer)
        copy.start()
        waiting.append(copy)
        return copy

    stages = len(ORDERS[0])
    source = [grad_ref.at[c] for c in range(chunks)]
    base = [0] * chunks
    length = [pieces] * chunks
    offsets = [[] for _ in range(chunks)]
    pending = [None] * chunks
    moves = []

    def spread(c, s):
        size, mine, peer = table[ORDERS[c % 2][s]]
        part = length[c] // size
        slots = bufs[s * 2 * chunks + 2 * c]
        pending[c] = [
            send(
                source[c].at[pl.ds(lax.rem(mine + k, size) * part, part)],
                slots.at[k - 1],
                peer(lax.rem(mine + k, size)),
            )
            for k in range(1, size)
        ]

    def gather(c, s):
        size, mine, peer = table[ORDERS[c % 2][s]]
        start, count = offsets[c][s]
        pending[c] = [
            send(
                sum_ref.at[c, pl.ds(start, count)],
                sum_ref.at[c, pl.ds(start, count)],
                peer(lax.rem(mine + k, size)),
            )
            for k in range(1, size)
        ]

    for c in range(chunks):
        spread(c, 0)
    for k, peer in enumerate(peers):
        copy = remote(
            enc_ref.at[pl.ds(peer[1] * frame_dev, frame_dev)],
            out_ref.at[:, pl.ds(me * cells, cells)],
            enc_send.at[k],
            enc_recv.at[k],
            peer,
        )
        copy.start()
        moves.append(copy)
    out_ref[:, pl.ds(me * cells, cells)] = enc_ref[pl.ds(me * frame_dev, frame_dev)]
    for s in range(stages):
        for c in range(chunks):
            size, mine, _ = table[ORDERS[c % 2][s]]
            part = length[c] // size
            slots, total = bufs[s * 2 * chunks + 2 * c : s * 2 * chunks + 2 * c + 2]
            value = source[c][pl.ds(mine * part, part)].astype(jnp.float32)
            for k, copy in enumerate(pending[c]):
                copy.wait_recv()
                value = value + slots[k].astype(jnp.float32)
            base[c] = base[c] + mine * part
            offsets[c].append((base[c], part))
            length[c] = part
            if s + 1 < stages:
                total[...] = value.astype(jnp.bfloat16)
                source[c] = total
                spread(c, s + 1)
            else:
                sum_ref[c, pl.ds(base[c], part)] = value.astype(jnp.bfloat16)
                gather(c, s)
    for s in range(stages - 1, -1, -1):
        for c in range(chunks):
            for copy in pending[c]:
                copy.wait_recv()
            if s > 0:
                gather(c, s - 1)
    for copy in waiting:
        copy.wait_send()
    for copy in moves:
        copy.wait()


def reduce_all(enc, grads, dps, tiles):
    frames, cells, channels = enc.shape
    chunks, pieces, rows, width = grads.shape
    vmem = pl.BlockSpec(memory_space=pltpu.VMEM)
    dma = pltpu.SemaphoreType.DMA
    scratch = []
    copies = 0
    for s in range(4):
        for c in range(chunks):
            sizes = group_sizes(ORDERS[c % 2], dps, tiles)
            part = pieces // math.prod(sizes[: s + 1])
            scratch.append(pltpu.VMEM((sizes[s] - 1, part, rows, width), jnp.bfloat16))
            scratch.append(pltpu.VMEM((part, rows, width), jnp.bfloat16))
            copies += 2 * (sizes[s] - 1)
    scratch += [dma((tiles - 1,)), dma((tiles - 1,)), dma((copies,)), dma((copies,))]
    return pl.pallas_call(
        functools.partial(reduce_kernel, dps, tiles),
        out_shape=[
            jax.ShapeDtypeStruct((frames // tiles, cells * tiles, channels), jnp.bfloat16),
            jax.ShapeDtypeStruct(grads.shape, jnp.bfloat16),
        ],
        in_specs=[vmem] * 2,
        out_specs=[vmem] * 2,
        scratch_shapes=scratch,
        compiler_params=pltpu.CompilerParams(
            collective_id=1, has_side_effects=True, vmem_limit_bytes=32 << 20
        ),
    )(enc, grads)


def contract_rows(left, right):
    return lax.dot_general(
        left, right, (((0,), (0,)), ((), ())), preferred_element_type=jnp.float32
    )


def patch_columns(padded, strip_rows, frame_width):
    pieces = [
        padded[:, i : i + strip_rows, j : j + frame_width, :]
        for i in range(3)
        for j in range(3)
    ]
    return jnp.concatenate(pieces, axis=-1).reshape(-1, 9 * padded.shape[-1])


def on_device(
    video_in, clip_lengths, norm_gain, norm_bias, spatial_weight, temporal_weight, cotangent
):
    dps, tiles = lax.axis_size("dp"), lax.axis_size("tile")
    _, frames, strip, width, channels = video_in.shape
    height = strip * tiles
    cells = strip * width
    frame_dev = frames // tiles
    tile = lax.axis_index("tile")
    video = video_in[0]
    top = video[:, 0].reshape(frames * width, channels)
    bot = video[:, strip - 1].reshape(frames * width, channels)
    stats, cot, above, below = exchange(
        video.reshape(frames, cells, channels),
        top,
        bot,
        cotangent[0].reshape(frame_dev, height * width, channels),
        tiles,
    )
    lengths = clip_lengths[0]
    clips = lengths.shape[0]
    upto = jnp.arange(clips)[:, None] >= jnp.arange(clips)[None, :]
    ends = jnp.sum(jnp.where(upto, lengths[None, :], 0), axis=1)
    ids = jnp.arange(frames, dtype=jnp.int32)
    clip_of = jnp.sum((ids[:, None] >= ends[None, :]).astype(jnp.int32), axis=1)
    same = clip_of[:, None] == clip_of[None, :]
    position = jnp.sum((same & (ids[None, :] < ids[:, None])).astype(jnp.int32), axis=1)
    member = same.astype(jnp.float32)
    per_group = channels // GROUPS
    count = jnp.sum(member, axis=1) * (height * width * per_group)

    def over_clip(part):
        return jnp.dot(member, part, precision=lax.Precision.HIGHEST) / count[:, None]

    mean = over_clip(stats[:frames, :GROUPS])
    var = jnp.maximum(over_clip(stats[frames:, :GROUPS]) - mean * mean, 0.0)
    mean_c = jnp.repeat(mean, per_group, axis=1)[:, None, None, :]
    rstd_c = jnp.repeat(lax.rsqrt(var + norm_eps), per_group, axis=1)[:, None, None, :]
    local_vals = video.astype(jnp.float32)
    halo = (frames, 1, width, channels)
    wide = jnp.concatenate([above.reshape(halo), video, below.reshape(halo)], axis=1)
    normed = (wide.astype(jnp.float32) - mean_c) * rstd_c * norm_gain + norm_bias
    row = jnp.arange(strip + 2) + tile * strip - 1
    inside = ((row >= 0) & (row < height))[None, :, None, None]
    active = jnp.where(inside, jax.nn.silu(normed), 0.0).astype(jnp.bfloat16)
    padded = jnp.pad(active, ((0, 0), (0, 0), (1, 1), (0, 0)))
    columns = patch_columns(padded, strip, width)
    conv_out = jnp.dot(
        columns, spatial_weight.reshape(9 * channels, channels), preferred_element_type=jnp.float32
    )
    block_out = (local_vals + conv_out.reshape(local_vals.shape)).astype(jnp.bfloat16)
    block_out = block_out.reshape(frames, cells, channels)

    earlier = []
    later = []
    for k in range(3):
        moved = jnp.pad(block_out, ((k, 0), (0, 0), (0, 0)))[:frames]
        earlier.append(jnp.where((position >= k)[:, None, None], moved, jnp.zeros_like(moved)))
        moved = jnp.pad(cot, ((0, k), (0, 0), (0, 0)))[k:]
        ahead = jnp.pad(position, (0, k))[k:]
        later.append(jnp.where((ahead >= k)[:, None, None], moved, jnp.zeros_like(moved)))
    earlier = jnp.concatenate(earlier, axis=-1).reshape(-1, 3 * channels)
    later = jnp.concatenate(later, axis=-1).reshape(-1, 3 * channels)
    lifted = jnp.dot(
        earlier, temporal_weight.reshape(3 * channels, channels), preferred_element_type=jnp.float32
    ).reshape(block_out.shape)
    encoded = (block_out.astype(jnp.float32) + lifted).astype(jnp.bfloat16)
    back_weight = jnp.transpose(temporal_weight, (0, 2, 1)).reshape(3 * channels, channels)
    pulled = jnp.dot(later, back_weight, preferred_element_type=jnp.float32).reshape(cot.shape)
    grad_block = (cot.astype(jnp.float32) + pulled).astype(jnp.bfloat16)
    temporal_term = contract_rows(earlier, cot.reshape(-1, channels))
    spatial_term = contract_rows(columns, grad_block.reshape(-1, channels))
    grads = jnp.concatenate([spatial_term, temporal_term], axis=0).astype(jnp.bfloat16)
    chunks = 6
    pieces = dps * tiles
    out, total = reduce_all(
        encoded,
        grads.reshape(chunks, pieces, 12 * channels // (chunks * pieces), channels),
        dps,
        tiles,
    )
    scale = 1.0 / math.sqrt(dps * frames * height * width)
    total = total.reshape(12, channels, channels).astype(jnp.float32) * scale
    return (
        out.reshape(1, frame_dev, height, width, channels),
        total[:9].reshape(3, 3, channels, channels),
        total[9:],
    )


def solution(mesh):
    return jax.shard_map(
        on_device,
        mesh=mesh,
        in_specs=(
            P("dp", None, "tile", None, None),
            P("dp", None),
            P(),
            P(),
            P(),
            P(),
            P("dp", "tile", None, None, None),
        ),
        out_specs=(P("dp", "tile", None, None, None), P(), P()),
        check_vma=False,
    )
```

```python
import functools
import math

import jax
import jax.numpy as jnp
from jax import lax
from jax.experimental import pallas as pl
from jax.experimental.pallas import tpu as pltpu
from jax.sharding import PartitionSpec as P

GROUPS = 32
MESH = pl.DeviceIdType.MESH
norm_eps = 1e-05


def remote(src, dst, send, recv, peer):
    return pltpu.make_async_remote_copy(
        src_ref=src,
        dst_ref=dst,
        send_sem=send,
        recv_sem=recv,
        device_id=peer,
        device_id_type=MESH,
    )


def digits(dps, tiles):
    dp, tile = lax.axis_index("dp"), lax.axis_index("tile")
    return {
        "core": (2, lax.rem(dp, 2), lambda j: ((dp // 2) * 2 + j, tile)),
        "y": (dps // 2, dp // 2, lambda j: (j * 2 + lax.rem(dp, 2), tile)),
        "lo": (2, lax.rem(tile, 2), lambda j: (dp, (tile // 2) * 2 + j)),
        "hi": (tiles // 2, tile // 2, lambda j: (dp, j * 2 + lax.rem(tile, 2))),
    }


ORDERS = (("core", "lo", "y", "hi"), ("core", "y", "lo", "hi"))


def group_sizes(order, dps, tiles):
    known = {"core": 2, "y": dps // 2, "lo": 2, "hi": tiles // 2}
    return [known[name] for name in order]


def pick_rows(lengths_ref, frame):
    clip, end = jnp.zeros_like(frame), 0
    for c in range(lengths_ref.shape[1]):
        end = end + lengths_ref[0, c]
        clip = clip + jnp.where(frame >= end, 1, 0)
    return clip


def dot32(a, b):
    return jnp.dot(
        a, b, precision=lax.Precision.HIGHEST, preferred_element_type=jnp.float32
    )


def contract(a, b, da, db):
    return lax.dot_general(
        a, b, (((da,), (db,)), ((), ())), preferred_element_type=jnp.float32
    )


def block_kernel(
    dps,
    tiles,
    width,
    lengths_ref,
    video_ref,
    strips_ref,
    cot_ref,
    gain_ref,
    bias_ref,
    sw_ref,
    tw_ref,
    out_ref,
    sum_ref,
    *scratch,
):
    scratch = list(scratch)
    mine, theirs, above, below, cot_rows, cols, early, late = scratch[:8]
    stat_send, stat_recv, halo_send, halo_recv, cot_send, cot_recv = scratch[8:14]
    enc_send, enc_recv, sends, recvs = scratch[14:18]
    bufs = scratch[18:]
    dp, me = lax.axis_index("dp"), lax.axis_index("tile")
    frames, cells, channels = video_ref.shape
    strip = cells // width
    height = strip * tiles
    rows = frames * cells
    frame_dev = cot_ref.shape[0]
    chunks, pieces = sum_ref.shape[:2]
    bf16, f32 = jnp.bfloat16, jnp.float32
    table = digits(dps, tiles)
    peers = [(dp, lax.rem(me + k, tiles)) for k in range(1, tiles)]
    greet = list(peers)
    for name in ("core", "y"):
        size, at, peer = table[name]
        greet += [peer(lax.rem(at + k, size)) for k in range(1, size)]
    barrier = pltpu.get_barrier_semaphore()
    for peer in greet:
        pl.semaphore_signal(barrier, inc=1, device_id=peer, device_id_type=MESH)

    values = video_ref[...].astype(f32)
    sums = jnp.concatenate(
        [jnp.sum(values, axis=1), jnp.sum(values * values, axis=1)], axis=0
    )
    lanes = mine.shape[1]
    per_group = channels // GROUPS
    member = lax.broadcasted_iota(jnp.int32, (channels, lanes), 0) // per_group
    group = lax.broadcasted_iota(jnp.int32, (channels, lanes), 1)
    mine[...] = dot32(sums, jnp.where(member == group, 1.0, 0.0).astype(f32))
    pl.semaphore_wait(barrier, len(greet))

    stats = []
    for k, peer in enumerate(peers):
        copy = remote(mine, theirs.at[k], stat_send.at[k], stat_recv.at[k], peer)
        copy.start()
        stats.append(copy)
    up = remote(strips_ref.at[:, 0], below, halo_send.at[0], halo_recv.at[0], (dp, me - 1))
    down = remote(
        strips_ref.at[:, strip - 1], above, halo_send.at[1], halo_recv.at[1], (dp, me + 1)
    )

    @pl.when(me > 0)
    def _():
        up.start()

    @pl.when(me < tiles - 1)
    def _():
        down.start()

    moves = []
    for k, peer in enumerate(peers):
        copy = remote(
            cot_ref.at[:, pl.ds(peer[1] * cells, cells)],
            cot_rows.at[pl.ds(me * frame_dev, frame_dev)],
            cot_send.at[k],
            cot_recv.at[k],
            peer,
        )
        copy.start()
        moves.append(copy)
    cot_rows[pl.ds(me * frame_dev, frame_dev)] = cot_ref[:, pl.ds(me * cells, cells)]

    clip_a = pick_rows(lengths_ref, lax.broadcasted_iota(jnp.int32, (frames, frames), 0))
    clip_b = pick_rows(lengths_ref, lax.broadcasted_iota(jnp.int32, (frames, frames), 1))
    same = jnp.where(clip_a == clip_b, 1.0, 0.0).astype(f32)
    count = jnp.sum(same, axis=1, keepdims=True) * (height * width * per_group)
    frame = lax.broadcasted_iota(jnp.int32, (rows, 1), 0) // cells
    clip = pick_rows(lengths_ref, frame)
    keeps = [None] + [
        jnp.where(
            jnp.logical_and(clip == pick_rows(lengths_ref, frame - k), frame >= k), 1.0, 0.0
        ).astype(f32)
        for k in (1, 2)
    ]
    member = lax.broadcasted_iota(jnp.int32, (lanes, channels), 1) // per_group
    group = lax.broadcasted_iota(jnp.int32, (lanes, channels), 0)
    widen = jnp.where(member == group, 1.0, 0.0).astype(f32)
    total = mine[...]
    for k, copy in enumerate(stats):
        copy.wait_recv()
        total = total + theirs[k]
    mean = dot32(same, total[:frames]) / count
    var = jnp.maximum(dot32(same, total[frames:]) / count - mean * mean, 0.0)
    mean = dot32(mean, widen)
    slope = dot32(lax.rsqrt(var + norm_eps), widen) * gain_ref[...]
    bias = bias_ref[...]

    @pl.when(me > 0)
    def _():
        down.wait_recv()

    @pl.when(me < tiles - 1)
    def _():
        up.wait_recv()

    ext = cells + 2 * width
    line = lax.broadcasted_iota(jnp.int32, (ext, channels), 0)
    row = line // width + me * strip - 1
    inside = jnp.logical_and(row >= 0, row < height)
    col = lax.rem(line, width)
    for f in range(frames):
        v = jnp.concatenate(
            [above[f].astype(f32), video_ref[f].astype(f32), below[f].astype(f32)], axis=0
        )
        v = (v - mean[f : f + 1]) * slope[f : f + 1] + bias
        v = jnp.where(inside, v / (1.0 + jnp.exp(-v)), 0.0)
        shifted = (
            jnp.where(col == 0, 0.0, pltpu.roll(v, 1, 0)),
            v,
            jnp.where(col == width - 1, 0.0, pltpu.roll(v, ext - 1, 0)),
        )
        for i in range(3):
            for j in range(3):
                tap = (i * 3 + j) * channels
                cols[f * cells : (f + 1) * cells, tap : tap + channels] = shifted[j][
                    i * width : i * width + cells
                ].astype(bf16)
    conv = jnp.dot(cols[...], sw_ref[...], preferred_element_type=f32)
    block = video_ref[...].astype(f32).reshape(rows, channels) + conv
    block = block.astype(bf16)
    early[:, :channels] = block
    block = block.astype(f32)
    for k in (1, 2):
        lag = k * cells
        span = slice(k * channels, (k + 1) * channels)
        early[:lag, span] = jnp.zeros((lag, channels), bf16)
        early[lag:, span] = (block[: rows - lag] * keeps[k][lag:]).astype(bf16)
    lifted = jnp.dot(early[...], tw_ref[...], preferred_element_type=f32)
    enc = bufs[0]
    enc[...] = (block + lifted).astype(bf16).reshape(frames, cells, channels)
    for k, peer in enumerate(peers):
        copy = remote(
            enc.at[pl.ds(peer[1] * frame_dev, frame_dev)],
            out_ref.at[:, pl.ds(me * cells, cells)],
            enc_send.at[k],
            enc_recv.at[k],
            peer,
        )
        copy.start()
        moves.append(copy)
    out_ref[:, pl.ds(me * cells, cells)] = enc[pl.ds(me * frame_dev, frame_dev)]

    for copy in moves[: tiles - 1]:
        copy.wait_recv()
    cot = cot_rows[...].reshape(rows, channels)
    cot32 = cot.astype(f32)
    late[:, :channels] = cot
    for k in (1, 2):
        lag = k * cells
        span = slice(k * channels, (k + 1) * channels)
        late[: rows - lag, span] = (cot32[lag:] * keeps[k][lag:]).astype(bf16)
        late[rows - lag :, span] = jnp.zeros((lag, channels), bf16)
    grad_block = cot32
    for k in range(3):
        span = slice(k * channels, (k + 1) * channels)
        grad_block = grad_block + contract(late[:, span], tw_ref[span, :], 1, 1)
    grad_block = grad_block.astype(bf16)

    sent = [0]
    waiting = []

    def send(src, dst, peer):
        at = sent[0]
        sent[0] += 1
        copy = remote(src, dst, sends.at[at], recvs.at[at], peer)
        copy.start()
        waiting.append(copy)
        return copy

    stages = len(ORDERS[0])
    narrow = bufs[1 : 1 + chunks]
    exact = bufs[1 + chunks : 1 + 2 * chunks]
    bufs = bufs[1 + 2 * chunks :]
    base = [0] * chunks
    length = [pieces] * chunks
    offsets = [[] for _ in range(chunks)]
    pending = [None] * chunks

    def spread(c, s):
        size, at, peer = table[ORDERS[c % 2][s]]
        part = length[c] // size
        slots = bufs[3 * (s * chunks + c)]
        pending[c] = [
            send(
                narrow[c].at[pl.ds(lax.rem(at + k, size) * part, part)],
                slots.at[k - 1],
                peer(lax.rem(at + k, size)),
            )
            for k in range(1, size)
        ]

    def gather(c, s):
        size, at, peer = table[ORDERS[c % 2][s]]
        start, number = offsets[c][s]
        here = sum_ref.at[c, pl.ds(start, number)]
        pending[c] = [
            send(here, here, peer(lax.rem(at + k, size))) for k in range(1, size)
        ]

    taps = 12 // chunks
    for c in range(chunks):
        parts = []
        for tap in range(c * taps, (c + 1) * taps):
            if tap < 9:
                left, right = cols[:, tap * channels : (tap + 1) * channels], grad_block
            else:
                left, right = early[:, (tap - 9) * channels : (tap - 8) * channels], cot
            parts.append(contract(left, right, 0, 0))
        value = jnp.concatenate(parts, axis=0).reshape(exact[c].shape)
        exact[c][...] = value
        narrow[c][...] = value.astype(bf16)
        spread(c, 0)
    for s in range(stages):
        for c in range(chunks):
            size, at, _ = table[ORDERS[c % 2][s]]
            part = length[c] // size
            slots, total16, total32 = bufs[3 * (s * chunks + c) : 3 * (s * chunks + c) + 3]
            value = exact[c][pl.ds(at * part, part)]
            for k, copy in enumerate(pending[c]):
                copy.wait_recv()
                value = value + slots[k].astype(f32)
            base[c] = base[c] + at * part
            offsets[c].append((base[c], part))
            length[c] = part
            if s + 1 < stages:
                total16[...] = value.astype(bf16)
                total32[...] = value
                narrow[c], exact[c] = total16, total32
                spread(c, s + 1)
            else:
                sum_ref[c, pl.ds(base[c], part)] = value.astype(bf16)
                gather(c, s)
    for s in range(stages - 1, -1, -1):
        for c in range(chunks):
            for copy in pending[c]:
                copy.wait_recv()
            if s > 0:
                gather(c, s - 1)

    @pl.when(me > 0)
    def _():
        up.wait_send()

    @pl.when(me < tiles - 1)
    def _():
        down.wait_send()

    for copy in stats[: tiles - 1] + moves + waiting:
        copy.wait_send()
    for copy in moves[tiles - 1 :]:
        copy.wait_recv()


def residual_block(lengths, video, strips, cot, gain, bias, sw, tw, dps, tiles, chunks):
    frames, cells, channels = video.shape
    width = strips.shape[2]
    pieces = dps * tiles
    depth = 12 * channels // (chunks * pieces)
    rows = frames * cells
    bf16, f32 = jnp.bfloat16, jnp.float32
    vmem = pl.BlockSpec(memory_space=pltpu.VMEM)
    dma = pltpu.SemaphoreType.DMA
    bufs = [pltpu.VMEM((frames, cells, channels), bf16)]
    bufs += [pltpu.VMEM((pieces, depth, channels), bf16)] * chunks
    bufs += [pltpu.VMEM((pieces, depth, channels), f32)] * chunks
    copies = 0
    for s in range(len(ORDERS[0])):
        for c in range(chunks):
            sizes = group_sizes(ORDERS[c % 2], dps, tiles)
            part = pieces // math.prod(sizes[: s + 1])
            bufs.append(pltpu.VMEM((sizes[s] - 1, part, depth, channels), bf16))
            bufs.append(pltpu.VMEM((part, depth, channels), bf16))
            bufs.append(pltpu.VMEM((part, depth, channels), f32))
            copies += 2 * (sizes[s] - 1)
    halo = pltpu.VMEM((frames, width, channels), bf16)
    scratch = [
        pltpu.VMEM((2 * frames, 128), f32),
        pltpu.VMEM((tiles - 1, 2 * frames, 128), f32),
        halo,
        halo,
        pltpu.VMEM((frames, cells, channels), bf16),
        pltpu.VMEM((rows, 9 * channels), bf16),
        pltpu.VMEM((rows, 3 * channels), bf16),
        pltpu.VMEM((rows, 3 * channels), bf16),
        dma((tiles - 1,)),
        dma((tiles - 1,)),
        dma((2,)),
        dma((2,)),
        dma((tiles - 1,)),
        dma((tiles - 1,)),
        dma((tiles - 1,)),
        dma((tiles - 1,)),
        dma((copies,)),
        dma((copies,)),
    ]
    return pl.pallas_call(
        functools.partial(block_kernel, dps, tiles, width),
        out_shape=[
            jax.ShapeDtypeStruct((frames // tiles, cells * tiles, channels), bf16),
            jax.ShapeDtypeStruct((chunks, pieces, depth, channels), bf16),
        ],
        in_specs=[
            pl.BlockSpec(memory_space=pltpu.SMEM),
            vmem,
            pl.BlockSpec(memory_space=pl.ANY),
            vmem,
            vmem,
            vmem,
            vmem,
            vmem,
        ],
        out_specs=[vmem] * 2,
        scratch_shapes=scratch + bufs,
        compiler_params=pltpu.CompilerParams(
            collective_id=0, has_side_effects=True, vmem_limit_bytes=48 << 20
        ),
    )(lengths, video, strips, cot, gain, bias, sw, tw)


def on_device(
    video_in, clip_lengths, norm_gain, norm_bias, spatial_weight, temporal_weight, cotangent
):
    dps, tiles = lax.axis_size("dp"), lax.axis_size("tile")
    _, frames, strip, width, channels = video_in.shape
    height = strip * tiles
    frame_dev = frames // tiles
    out, total = residual_block(
        clip_lengths,
        video_in[0].reshape(frames, strip * width, channels),
        video_in[0],
        cotangent[0].reshape(frame_dev, height * width, channels),
        norm_gain[None],
        norm_bias[None],
        spatial_weight.reshape(9 * channels, channels),
        temporal_weight.reshape(3 * channels, channels),
        dps,
        tiles,
        6,
    )
    scale = 1.0 / math.sqrt(dps * frames * height * width)
    total = total.reshape(12 * channels, channels)
    spatial, temporal = lax.optimization_barrier(
        (total[: 9 * channels], total[9 * channels :])
    )
    return (
        out.reshape(1, frame_dev, height, width, channels),
        (spatial.astype(jnp.float32) * scale).reshape(3, 3, channels, channels),
        (temporal.astype(jnp.float32) * scale).reshape(3, channels, channels),
    )


def solution(mesh):
    return jax.shard_map(
        on_device,
        mesh=mesh,
        in_specs=(
            P("dp", None, "tile", None, None),
            P("dp", None),
            P(),
            P(),
            P(),
            P(),
            P("dp", "tile", None, None, None),
        ),
        out_specs=(P("dp", "tile", None, None, None), P(), P()),
        check_vma=False,
    )
```

```python
import functools
import math

import jax
import jax.numpy as jnp
from jax import lax
from jax.experimental import pallas as pl
from jax.experimental.pallas import tpu as pltpu
from jax.sharding import PartitionSpec as P

GROUPS = 32
MESH = pl.DeviceIdType.MESH
norm_eps = 1e-05


def remote(src, dst, send, recv, peer):
    return pltpu.make_async_remote_copy(
        src_ref=src,
        dst_ref=dst,
        send_sem=send,
        recv_sem=recv,
        device_id=peer,
        device_id_type=MESH,
    )


def digits(dps, tiles):
    dp, tile = lax.axis_index("dp"), lax.axis_index("tile")
    return {
        "core": (2, lax.rem(dp, 2), lambda j: ((dp // 2) * 2 + j, tile)),
        "y": (dps // 2, dp // 2, lambda j: (j * 2 + lax.rem(dp, 2), tile)),
        "lo": (2, lax.rem(tile, 2), lambda j: (dp, (tile // 2) * 2 + j)),
        "hi": (tiles // 2, tile // 2, lambda j: (dp, j * 2 + lax.rem(tile, 2))),
    }


ORDERS = (("core", "lo", "y", "hi"), ("core", "y", "lo", "hi"))


def group_sizes(order, dps, tiles):
    known = {"core": 2, "y": dps // 2, "lo": 2, "hi": tiles // 2}
    return [known[name] for name in order]


def pick_rows(lengths_ref, frame):
    clip, end = jnp.zeros_like(frame), 0
    for c in range(lengths_ref.shape[1]):
        end = end + lengths_ref[0, c]
        clip = clip + jnp.where(frame >= end, 1, 0)
    return clip


def dot32(a, b):
    return jnp.dot(
        a, b, precision=lax.Precision.HIGHEST, preferred_element_type=jnp.float32
    )


def contract(a, b, da, db):
    return lax.dot_general(
        a, b, (((da,), (db,)), ((), ())), preferred_element_type=jnp.float32
    )


def block_kernel(
    dps,
    tiles,
    width,
    lengths_ref,
    video_hbm,
    strips_ref,
    cot_ref,
    gain_hbm,
    bias_hbm,
    sw_hbm,
    tw_hbm,
    out_ref,
    sum_ref,
    *scratch,
):
    scratch = list(scratch)
    mine, theirs, above, below, cot_rows, cols, early, late = scratch[:8]
    stat_send, stat_recv, halo_send, halo_recv, cot_send, cot_recv = scratch[8:14]
    enc_send, enc_recv, sends, recvs = scratch[14:18]
    video_ref, gain_ref, bias_ref, sw_ref, tw_ref, load_sem = scratch[18:24]
    bufs = scratch[24:]
    dp, me = lax.axis_index("dp"), lax.axis_index("tile")
    frames, cells, channels = video_ref.shape
    strip = cells // width
    height = strip * tiles
    rows = frames * cells
    frame_dev = cot_ref.shape[0]
    chunks, pieces = sum_ref.shape[:2]
    bf16, f32 = jnp.bfloat16, jnp.float32
    table = digits(dps, tiles)
    peers = [(dp, lax.rem(me + k, tiles)) for k in range(1, tiles)]
    greet = list(peers)
    for name in ("core", "y"):
        size, at, peer = table[name]
        greet += [peer(lax.rem(at + k, size)) for k in range(1, size)]
    barrier = pltpu.get_barrier_semaphore()
    for peer in greet:
        pl.semaphore_signal(barrier, inc=1, device_id=peer, device_id_type=MESH)

    loads = [
        pltpu.make_async_copy(src, dst, load_sem.at[k])
        for k, (src, dst) in enumerate(
            (
                (video_hbm, video_ref),
                (gain_hbm, gain_ref),
                (bias_hbm, bias_ref),
                (sw_hbm, sw_ref),
                (tw_hbm, tw_ref),
                (
                    cot_ref.at[:, pl.ds(me * cells, cells)],
                    cot_rows.at[pl.ds(me * frame_dev, frame_dev)],
                ),
            )
        )
    ]
    for copy in loads:
        copy.start()
    loads[0].wait()
    values = video_ref[...].astype(f32)
    sums = jnp.concatenate(
        [jnp.sum(values, axis=1), jnp.sum(values * values, axis=1)], axis=0
    )
    lanes = mine.shape[1]
    per_group = channels // GROUPS
    member = lax.broadcasted_iota(jnp.int32, (channels, lanes), 0) // per_group
    group = lax.broadcasted_iota(jnp.int32, (channels, lanes), 1)
    mine[...] = dot32(sums, jnp.where(member == group, 1.0, 0.0).astype(f32))
    pl.semaphore_wait(barrier, len(greet))

    stats = []
    for k, peer in enumerate(peers):
        copy = remote(mine, theirs.at[k], stat_send.at[k], stat_recv.at[k], peer)
        copy.start()
        stats.append(copy)
    up = remote(strips_ref.at[:, 0], below, halo_send.at[0], halo_recv.at[0], (dp, me - 1))
    down = remote(
        strips_ref.at[:, strip - 1], above, halo_send.at[1], halo_recv.at[1], (dp, me + 1)
    )

    @pl.when(me > 0)
    def _():
        up.start()

    @pl.when(me < tiles - 1)
    def _():
        down.start()

    moves = []
    for k, peer in enumerate(peers):
        copy = remote(
            cot_ref.at[:, pl.ds(peer[1] * cells, cells)],
            cot_rows.at[pl.ds(me * frame_dev, frame_dev)],
            cot_send.at[k],
            cot_recv.at[k],
            peer,
        )
        copy.start()
        moves.append(copy)

    clip_a = pick_rows(lengths_ref, lax.broadcasted_iota(jnp.int32, (frames, frames), 0))
    clip_b = pick_rows(lengths_ref, lax.broadcasted_iota(jnp.int32, (frames, frames), 1))
    same = jnp.where(clip_a == clip_b, 1.0, 0.0).astype(f32)
    count = jnp.sum(same, axis=1, keepdims=True) * (height * width * per_group)
    frame = lax.broadcasted_iota(jnp.int32, (rows, 1), 0) // cells
    clip = pick_rows(lengths_ref, frame)
    keeps = [None] + [
        jnp.where(
            jnp.logical_and(clip == pick_rows(lengths_ref, frame - k), frame >= k), 1.0, 0.0
        ).astype(f32)
        for k in (1, 2)
    ]
    member = lax.broadcasted_iota(jnp.int32, (lanes, channels), 1) // per_group
    group = lax.broadcasted_iota(jnp.int32, (lanes, channels), 0)
    widen = jnp.where(member == group, 1.0, 0.0).astype(f32)
    total = mine[...]
    for k, copy in enumerate(stats):
        copy.wait_recv()
        total = total + theirs[k]
    mean = dot32(same, total[:frames]) / count
    var = jnp.maximum(dot32(same, total[frames:]) / count - mean * mean, 0.0)
    loads[1].wait()
    loads[2].wait()
    mean = dot32(mean, widen)
    slope = dot32(lax.rsqrt(var + norm_eps), widen) * gain_ref[...]
    bias = bias_ref[...]

    @pl.when(me > 0)
    def _():
        down.wait_recv()

    @pl.when(me < tiles - 1)
    def _():
        up.wait_recv()

    ext = cells + 2 * width
    line = lax.broadcasted_iota(jnp.int32, (ext, channels), 0)
    row = line // width + me * strip - 1
    inside = jnp.logical_and(row >= 0, row < height)
    col = lax.rem(line, width)
    for f in range(frames):
        v = jnp.concatenate(
            [above[f].astype(f32), video_ref[f].astype(f32), below[f].astype(f32)], axis=0
        )
        v = (v - mean[f : f + 1]) * slope[f : f + 1] + bias
        v = jnp.where(inside, v / (1.0 + jnp.exp(-v)), 0.0)
        shifted = (
            jnp.where(col == 0, 0.0, pltpu.roll(v, 1, 0)),
            v,
            jnp.where(col == width - 1, 0.0, pltpu.roll(v, ext - 1, 0)),
        )
        for i in range(3):
            for j in range(3):
                tap = (i * 3 + j) * channels
                cols[f * cells : (f + 1) * cells, tap : tap + channels] = shifted[j][
                    i * width : i * width + cells
                ].astype(bf16)
    loads[3].wait()
    conv = jnp.dot(cols[...], sw_ref[...], preferred_element_type=f32)
    block = video_ref[...].astype(f32).reshape(rows, channels) + conv
    block = block.astype(bf16)
    early[:, :channels] = block
    block = block.astype(f32)
    for k in (1, 2):
        lag = k * cells
        span = slice(k * channels, (k + 1) * channels)
        early[:lag, span] = jnp.zeros((lag, channels), bf16)
        early[lag:, span] = (block[: rows - lag] * keeps[k][lag:]).astype(bf16)
    loads[4].wait()
    lifted = jnp.dot(early[...], tw_ref[...], preferred_element_type=f32)
    enc = bufs[0]
    enc[...] = (block + lifted).astype(bf16).reshape(frames, cells, channels)
    for k, peer in enumerate(peers):
        copy = remote(
            enc.at[pl.ds(peer[1] * frame_dev, frame_dev)],
            out_ref.at[:, pl.ds(me * cells, cells)],
            enc_send.at[k],
            enc_recv.at[k],
            peer,
        )
        copy.start()
        moves.append(copy)
    out_ref[:, pl.ds(me * cells, cells)] = enc[pl.ds(me * frame_dev, frame_dev)]

    loads[5].wait()
    for copy in moves[: tiles - 1]:
        copy.wait_recv()
    cot = cot_rows[...].reshape(rows, channels)
    cot32 = cot.astype(f32)
    late[:, :channels] = cot
    for k in (1, 2):
        lag = k * cells
        span = slice(k * channels, (k + 1) * channels)
        late[: rows - lag, span] = (cot32[lag:] * keeps[k][lag:]).astype(bf16)
        late[rows - lag :, span] = jnp.zeros((lag, channels), bf16)
    grad_block = cot32
    for k in range(3):
        span = slice(k * channels, (k + 1) * channels)
        grad_block = grad_block + contract(late[:, span], tw_ref[span, :], 1, 1)
    grad_block = grad_block.astype(bf16)

    sent = [0]
    waiting = []

    def send(src, dst, peer):
        at = sent[0]
        sent[0] += 1
        copy = remote(src, dst, sends.at[at], recvs.at[at], peer)
        copy.start()
        waiting.append(copy)
        return copy

    stages = len(ORDERS[0])
    narrow = bufs[1 : 1 + chunks]
    exact = bufs[1 + chunks : 1 + 2 * chunks]
    bufs = bufs[1 + 2 * chunks :]
    base = [0] * chunks
    length = [pieces] * chunks
    offsets = [[] for _ in range(chunks)]
    pending = [None] * chunks

    def spread(c, s):
        size, at, peer = table[ORDERS[c % 2][s]]
        part = length[c] // size
        slots = bufs[3 * (s * chunks + c)]
        pending[c] = [
            send(
                narrow[c].at[pl.ds(lax.rem(at + k, size) * part, part)],
                slots.at[k - 1],
                peer(lax.rem(at + k, size)),
            )
            for k in range(1, size)
        ]

    def gather(c, s):
        size, at, peer = table[ORDERS[c % 2][s]]
        start, number = offsets[c][s]
        here = sum_ref.at[c, pl.ds(start, number)]
        pending[c] = [
            send(here, here, peer(lax.rem(at + k, size))) for k in range(1, size)
        ]

    taps = 12 // chunks
    for c in range(chunks):
        parts = []
        for tap in range(c * taps, (c + 1) * taps):
            if tap < 9:
                left, right = cols[:, tap * channels : (tap + 1) * channels], grad_block
            else:
                left, right = early[:, (tap - 9) * channels : (tap - 8) * channels], cot
            parts.append(contract(left, right, 0, 0))
        value = jnp.concatenate(parts, axis=0).reshape(exact[c].shape)
        exact[c][...] = value
        narrow[c][...] = value.astype(bf16)
        spread(c, 0)
    for s in range(stages):
        for c in range(chunks):
            size, at, _ = table[ORDERS[c % 2][s]]
            part = length[c] // size
            slots, total16, total32 = bufs[3 * (s * chunks + c) : 3 * (s * chunks + c) + 3]
            value = exact[c][pl.ds(at * part, part)]
            for k, copy in enumerate(pending[c]):
                copy.wait_recv()
                value = value + slots[k].astype(f32)
            base[c] = base[c] + at * part
            offsets[c].append((base[c], part))
            length[c] = part
            if s + 1 < stages:
                total16[...] = value.astype(bf16)
                total32[...] = value
                narrow[c], exact[c] = total16, total32
                spread(c, s + 1)
            else:
                sum_ref[c, pl.ds(base[c], part)] = value.astype(bf16)
                gather(c, s)
    for s in range(stages - 1, -1, -1):
        for c in range(chunks):
            for copy in pending[c]:
                copy.wait_recv()
            if s > 0:
                gather(c, s - 1)

    @pl.when(me > 0)
    def _():
        up.wait_send()

    @pl.when(me < tiles - 1)
    def _():
        down.wait_send()

    for copy in stats[: tiles - 1] + moves + waiting:
        copy.wait_send()
    for copy in moves[tiles - 1 :]:
        copy.wait_recv()


def residual_block(lengths, video, strips, cot, gain, bias, sw, tw, dps, tiles, chunks):
    frames, cells, channels = video.shape
    width = strips.shape[2]
    pieces = dps * tiles
    depth = 12 * channels // (chunks * pieces)
    rows = frames * cells
    bf16, f32 = jnp.bfloat16, jnp.float32
    vmem = pl.BlockSpec(memory_space=pltpu.VMEM)
    dma = pltpu.SemaphoreType.DMA
    bufs = [pltpu.VMEM((frames, cells, channels), bf16)]
    bufs += [pltpu.VMEM((pieces, depth, channels), bf16)] * chunks
    bufs += [pltpu.VMEM((pieces, depth, channels), f32)] * chunks
    copies = 0
    for s in range(len(ORDERS[0])):
        for c in range(chunks):
            sizes = group_sizes(ORDERS[c % 2], dps, tiles)
            part = pieces // math.prod(sizes[: s + 1])
            bufs.append(pltpu.VMEM((sizes[s] - 1, part, depth, channels), bf16))
            bufs.append(pltpu.VMEM((part, depth, channels), bf16))
            bufs.append(pltpu.VMEM((part, depth, channels), f32))
            copies += 2 * (sizes[s] - 1)
    halo = pltpu.VMEM((frames, width, channels), bf16)
    scratch = [
        pltpu.VMEM((2 * frames, 128), f32),
        pltpu.VMEM((tiles - 1, 2 * frames, 128), f32),
        halo,
        halo,
        pltpu.VMEM((frames, cells, channels), bf16),
        pltpu.VMEM((rows, 9 * channels), bf16),
        pltpu.VMEM((rows, 3 * channels), bf16),
        pltpu.VMEM((rows, 3 * channels), bf16),
        dma((tiles - 1,)),
        dma((tiles - 1,)),
        dma((2,)),
        dma((2,)),
        dma((tiles - 1,)),
        dma((tiles - 1,)),
        dma((tiles - 1,)),
        dma((tiles - 1,)),
        dma((copies,)),
        dma((copies,)),
        pltpu.VMEM(video.shape, bf16),
        pltpu.VMEM(gain.shape, f32),
        pltpu.VMEM(bias.shape, f32),
        pltpu.VMEM(sw.shape, bf16),
        pltpu.VMEM(tw.shape, bf16),
        dma((6,)),
    ]
    return pl.pallas_call(
        functools.partial(block_kernel, dps, tiles, width),
        out_shape=[
            jax.ShapeDtypeStruct((frames // tiles, cells * tiles, channels), bf16),
            jax.ShapeDtypeStruct((chunks, pieces, depth, channels), bf16),
        ],
        in_specs=[pl.BlockSpec(memory_space=pltpu.SMEM)]
        + [pl.BlockSpec(memory_space=pl.ANY)] * 7,
        out_specs=[vmem] * 2,
        scratch_shapes=scratch + bufs,
        compiler_params=pltpu.CompilerParams(
            collective_id=0, has_side_effects=True, vmem_limit_bytes=56 << 20
        ),
    )(lengths, video, strips, cot, gain, bias, sw, tw)


def on_device(
    video_in, clip_lengths, norm_gain, norm_bias, spatial_weight, temporal_weight, cotangent
):
    dps, tiles = lax.axis_size("dp"), lax.axis_size("tile")
    _, frames, strip, width, channels = video_in.shape
    height = strip * tiles
    frame_dev = frames // tiles
    out, total = residual_block(
        clip_lengths,
        video_in[0].reshape(frames, strip * width, channels),
        video_in[0],
        cotangent[0].reshape(frame_dev, height * width, channels),
        norm_gain[None],
        norm_bias[None],
        spatial_weight.reshape(9 * channels, channels),
        temporal_weight.reshape(3 * channels, channels),
        dps,
        tiles,
        6,
    )
    scale = 1.0 / math.sqrt(dps * frames * height * width)
    total = total.reshape(12 * channels, channels)
    spatial, temporal = lax.optimization_barrier(
        (total[: 9 * channels], total[9 * channels :])
    )
    return (
        out.reshape(1, frame_dev, height, width, channels),
        (spatial.astype(jnp.float32) * scale).reshape(3, 3, channels, channels),
        (temporal.astype(jnp.float32) * scale).reshape(3, channels, channels),
    )


def solution(mesh):
    return jax.shard_map(
        on_device,
        mesh=mesh,
        in_specs=(
            P("dp", None, "tile", None, None),
            P("dp", None),
            P(),
            P(),
            P(),
            P(),
            P("dp", "tile", None, None, None),
        ),
        out_specs=(P("dp", "tile", None, None, None), P(), P()),
        check_vma=False,
    )
```

```python
import functools
import math

import jax
import jax.numpy as jnp
from jax import lax
from jax.experimental import pallas as pl
from jax.experimental.pallas import tpu as pltpu
from jax.sharding import PartitionSpec as P

GROUPS = 32
MESH = pl.DeviceIdType.MESH
norm_eps = 1e-05


def remote(src, dst, send, recv, peer):
    return pltpu.make_async_remote_copy(
        src_ref=src,
        dst_ref=dst,
        send_sem=send,
        recv_sem=recv,
        device_id=peer,
        device_id_type=MESH,
    )


def digits(dps, tiles):
    dp, tile = lax.axis_index("dp"), lax.axis_index("tile")
    return {
        "core": (2, lax.rem(dp, 2), lambda j: ((dp // 2) * 2 + j, tile)),
        "y": (dps // 2, dp // 2, lambda j: (j * 2 + lax.rem(dp, 2), tile)),
        "lo": (2, lax.rem(tile, 2), lambda j: (dp, (tile // 2) * 2 + j)),
        "hi": (tiles // 2, tile // 2, lambda j: (dp, j * 2 + lax.rem(tile, 2))),
    }


ORDERS = (("core", "lo", "y", "hi"), ("core", "y", "lo", "hi"))


def group_sizes(order, dps, tiles):
    known = {"core": 2, "y": dps // 2, "lo": 2, "hi": tiles // 2}
    return [known[name] for name in order]


def pick_rows(lengths_ref, frame):
    clip, end = jnp.zeros_like(frame), 0
    for c in range(lengths_ref.shape[1]):
        end = end + lengths_ref[0, c]
        clip = clip + jnp.where(frame >= end, 1, 0)
    return clip


def dot32(a, b):
    return jnp.dot(
        a, b, precision=lax.Precision.HIGHEST, preferred_element_type=jnp.float32
    )


def contract(a, b, da, db):
    return lax.dot_general(
        a, b, (((da,), (db,)), ((), ())), preferred_element_type=jnp.float32
    )


def block_kernel(
    dps,
    tiles,
    width,
    lengths_ref,
    video_hbm,
    strips_ref,
    cot_ref,
    gain_hbm,
    bias_hbm,
    sw_hbm,
    tw_hbm,
    out_ref,
    sum_ref,
    *scratch,
):
    scratch = list(scratch)
    mine, theirs, above, below, cot_rows, cols, early, late = scratch[:8]
    stat_send, stat_recv, halo_send, halo_recv, cot_send, cot_recv = scratch[8:14]
    enc_send, enc_recv, sends, recvs = scratch[14:18]
    video_ref, gain_ref, bias_ref, sw_ref, tw_ref, load_sem = scratch[18:24]
    bufs = scratch[24:]
    dp, me = lax.axis_index("dp"), lax.axis_index("tile")
    frames, cells, channels = video_ref.shape
    strip = cells // width
    height = strip * tiles
    rows = frames * cells
    frame_dev = cot_ref.shape[0]
    chunks, pieces = sum_ref.shape[:2]
    bf16, f32 = jnp.bfloat16, jnp.float32
    table = digits(dps, tiles)
    peers = [(dp, lax.rem(me + k, tiles)) for k in range(1, tiles)]
    greet = list(peers)
    for name in ("core", "y"):
        size, at, peer = table[name]
        greet += [peer(lax.rem(at + k, size)) for k in range(1, size)]
    barrier = pltpu.get_barrier_semaphore()
    for peer in greet:
        pl.semaphore_signal(barrier, inc=1, device_id=peer, device_id_type=MESH)

    loads = [
        pltpu.make_async_copy(src, dst, load_sem.at[k])
        for k, (src, dst) in enumerate(
            (
                (video_hbm, video_ref),
                (gain_hbm, gain_ref),
                (bias_hbm, bias_ref),
                (sw_hbm, sw_ref),
                (tw_hbm, tw_ref),
                (
                    cot_ref.at[:, pl.ds(me * cells, cells)],
                    cot_rows.at[pl.ds(me * frame_dev, frame_dev)],
                ),
            )
        )
    ]
    for copy in loads:
        copy.start()
    loads[0].wait()
    values = video_ref[...].astype(f32)
    sums = jnp.concatenate(
        [jnp.sum(values, axis=1), jnp.sum(values * values, axis=1)], axis=0
    )
    lanes = mine.shape[1]
    per_group = channels // GROUPS
    member = lax.broadcasted_iota(jnp.int32, (channels, lanes), 0) // per_group
    group = lax.broadcasted_iota(jnp.int32, (channels, lanes), 1)
    mine[...] = dot32(sums, jnp.where(member == group, 1.0, 0.0).astype(f32))
    pl.semaphore_wait(barrier, len(greet))

    stats = []
    for k, peer in enumerate(peers):
        copy = remote(mine, theirs.at[k], stat_send.at[k], stat_recv.at[k], peer)
        copy.start()
        stats.append(copy)
    up = remote(strips_ref.at[:, 0], below, halo_send.at[0], halo_recv.at[0], (dp, me - 1))
    down = remote(
        strips_ref.at[:, strip - 1], above, halo_send.at[1], halo_recv.at[1], (dp, me + 1)
    )

    @pl.when(me > 0)
    def _():
        up.start()

    @pl.when(me < tiles - 1)
    def _():
        down.start()

    moves = []
    for k, peer in enumerate(peers):
        copy = remote(
            cot_ref.at[:, pl.ds(peer[1] * cells, cells)],
            cot_rows.at[pl.ds(me * frame_dev, frame_dev)],
            cot_send.at[k],
            cot_recv.at[k],
            peer,
        )
        copy.start()
        moves.append(copy)

    clip_a = pick_rows(lengths_ref, lax.broadcasted_iota(jnp.int32, (frames, frames), 0))
    clip_b = pick_rows(lengths_ref, lax.broadcasted_iota(jnp.int32, (frames, frames), 1))
    same = jnp.where(clip_a == clip_b, 1.0, 0.0).astype(f32)
    count = jnp.sum(same, axis=1, keepdims=True) * (height * width * per_group)
    frame = lax.broadcasted_iota(jnp.int32, (rows, 1), 0) // cells
    clip = pick_rows(lengths_ref, frame)
    keeps = [None] + [
        jnp.where(
            jnp.logical_and(clip == pick_rows(lengths_ref, frame - k), frame >= k), 1.0, 0.0
        ).astype(f32)
        for k in (1, 2)
    ]
    member = lax.broadcasted_iota(jnp.int32, (lanes, channels), 1) // per_group
    group = lax.broadcasted_iota(jnp.int32, (lanes, channels), 0)
    widen = jnp.where(member == group, 1.0, 0.0).astype(f32)
    total = mine[...]
    for k, copy in enumerate(stats):
        copy.wait_recv()
        total = total + theirs[k]
    mean = dot32(same, total[:frames]) / count
    var = jnp.maximum(dot32(same, total[frames:]) / count - mean * mean, 0.0)
    loads[1].wait()
    loads[2].wait()
    mean = dot32(mean, widen)
    slope = dot32(lax.rsqrt(var + norm_eps), widen) * gain_ref[...]
    bias = bias_ref[...]

    @pl.when(me > 0)
    def _():
        down.wait_recv()

    @pl.when(me < tiles - 1)
    def _():
        up.wait_recv()

    ext = cells + 2 * width
    line = lax.broadcasted_iota(jnp.int32, (ext, channels), 0)
    row = line // width + me * strip - 1
    inside = jnp.logical_and(row >= 0, row < height)
    col = lax.rem(line, width)
    for f in range(frames):
        v = jnp.concatenate(
            [above[f].astype(f32), video_ref[f].astype(f32), below[f].astype(f32)], axis=0
        )
        v = (v - mean[f : f + 1]) * slope[f : f + 1] + bias
        v = jnp.where(inside, v / (1.0 + jnp.exp(-v)), 0.0)
        shifted = (
            jnp.where(col == 0, 0.0, pltpu.roll(v, 1, 0)),
            v,
            jnp.where(col == width - 1, 0.0, pltpu.roll(v, ext - 1, 0)),
        )
        for i in range(3):
            for j in range(3):
                tap = (i * 3 + j) * channels
                cols[f * cells : (f + 1) * cells, tap : tap + channels] = shifted[j][
                    i * width : i * width + cells
                ].astype(bf16)
    loads[3].wait()
    conv = jnp.dot(cols[...], sw_ref[...], preferred_element_type=f32)
    block = video_ref[...].astype(f32).reshape(rows, channels) + conv
    block = block.astype(bf16)
    early[:, :channels] = block
    block = block.astype(f32)
    for k in (1, 2):
        lag = k * cells
        span = slice(k * channels, (k + 1) * channels)
        early[:lag, span] = jnp.zeros((lag, channels), bf16)
        early[lag:, span] = (block[: rows - lag] * keeps[k][lag:]).astype(bf16)
    loads[4].wait()
    lifted = jnp.dot(early[...], tw_ref[...], preferred_element_type=f32)
    enc = bufs[0]
    enc[...] = (block + lifted).astype(bf16).reshape(frames, cells, channels)
    for k, peer in enumerate(peers):
        copy = remote(
            enc.at[pl.ds(peer[1] * frame_dev, frame_dev)],
            out_ref.at[:, pl.ds(me * cells, cells)],
            enc_send.at[k],
            enc_recv.at[k],
            peer,
        )
        copy.start()
        moves.append(copy)
    out_ref[:, pl.ds(me * cells, cells)] = enc[pl.ds(me * frame_dev, frame_dev)]

    loads[5].wait()
    for copy in moves[: tiles - 1]:
        copy.wait_recv()
    cot = cot_rows[...].reshape(rows, channels)
    cot32 = cot.astype(f32)
    late[:, :channels] = cot
    for k in (1, 2):
        lag = k * cells
        span = slice(k * channels, (k + 1) * channels)
        late[: rows - lag, span] = (cot32[lag:] * keeps[k][lag:]).astype(bf16)
        late[rows - lag :, span] = jnp.zeros((lag, channels), bf16)
    grad_block = cot32
    for k in range(3):
        span = slice(k * channels, (k + 1) * channels)
        grad_block = grad_block + contract(late[:, span], tw_ref[span, :], 1, 1)
    grad_block = grad_block.astype(bf16)

    sent = [0]
    waiting = []

    def send(src, dst, peer):
        at = sent[0]
        sent[0] += 1
        copy = remote(src, dst, sends.at[at], recvs.at[at], peer)
        copy.start()
        waiting.append(copy)
        return copy

    stages = len(ORDERS[0])
    narrow = bufs[1 : 1 + chunks]
    exact = bufs[1 + chunks : 1 + 2 * chunks]
    bufs = bufs[1 + 2 * chunks :]
    base = [0] * chunks
    length = [pieces] * chunks
    offsets = [[] for _ in range(chunks)]
    pending = [None] * chunks

    def spread(c, s):
        size, at, peer = table[ORDERS[c % 2][s]]
        part = length[c] // size
        slots = bufs[3 * (s * chunks + c)]
        pending[c] = [
            send(
                narrow[c].at[pl.ds(lax.rem(at + k, size) * part, part)],
                slots.at[k - 1],
                peer(lax.rem(at + k, size)),
            )
            for k in range(1, size)
        ]

    def gather(c, s):
        size, at, peer = table[ORDERS[c % 2][s]]
        start, number = offsets[c][s]
        here = sum_ref.at[c, pl.ds(start, number)]
        pending[c] = [
            send(here, here, peer(lax.rem(at + k, size))) for k in range(1, size)
        ]

    taps = 12 // chunks
    for c in range(chunks):
        parts = []
        for tap in range(c * taps, (c + 1) * taps):
            if tap < 9:
                left, right = cols[:, tap * channels : (tap + 1) * channels], grad_block
            else:
                left, right = early[:, (tap - 9) * channels : (tap - 8) * channels], cot
            parts.append(contract(left, right, 0, 0))
        value = jnp.concatenate(parts, axis=0).reshape(exact[c].shape)
        exact[c][...] = value
        narrow[c][...] = value.astype(bf16)
        spread(c, 0)
    for s in range(stages):
        for c in range(chunks):
            size, at, _ = table[ORDERS[c % 2][s]]
            part = length[c] // size
            slots, total16, total32 = bufs[3 * (s * chunks + c) : 3 * (s * chunks + c) + 3]
            value = exact[c][pl.ds(at * part, part)]
            for k, copy in enumerate(pending[c]):
                copy.wait_recv()
                value = value + slots[k].astype(f32)
            base[c] = base[c] + at * part
            offsets[c].append((base[c], part))
            length[c] = part
            if s + 1 < stages:
                total16[...] = value.astype(bf16)
                total32[...] = value
                narrow[c], exact[c] = total16, total32
                spread(c, s + 1)
            else:
                sum_ref[c, pl.ds(base[c], part)] = value.astype(bf16)
                gather(c, s)
    for s in range(stages - 1, -1, -1):
        for c in range(chunks):
            for copy in pending[c]:
                copy.wait_recv()
            if s > 0:
                gather(c, s - 1)

    @pl.when(me > 0)
    def _():
        up.wait_send()

    @pl.when(me < tiles - 1)
    def _():
        down.wait_send()

    for copy in stats[: tiles - 1] + moves + waiting:
        copy.wait_send()
    for copy in moves[tiles - 1 :]:
        copy.wait_recv()


def residual_block(lengths, video, strips, cot, gain, bias, sw, tw, dps, tiles, chunks):
    frames, cells, channels = video.shape
    width = strips.shape[2]
    pieces = dps * tiles
    depth = 12 * channels // (chunks * pieces)
    rows = frames * cells
    bf16, f32 = jnp.bfloat16, jnp.float32
    vmem = pl.BlockSpec(memory_space=pltpu.VMEM)
    dma = pltpu.SemaphoreType.DMA
    bufs = [pltpu.VMEM((frames, cells, channels), bf16)]
    bufs += [pltpu.VMEM((pieces, depth, channels), bf16)] * chunks
    bufs += [pltpu.VMEM((pieces, depth, channels), f32)] * chunks
    copies = 0
    for s in range(len(ORDERS[0])):
        for c in range(chunks):
            sizes = group_sizes(ORDERS[c % 2], dps, tiles)
            part = pieces // math.prod(sizes[: s + 1])
            bufs.append(pltpu.VMEM((sizes[s] - 1, part, depth, channels), bf16))
            bufs.append(pltpu.VMEM((part, depth, channels), bf16))
            bufs.append(pltpu.VMEM((part, depth, channels), f32))
            copies += 2 * (sizes[s] - 1)
    halo = pltpu.VMEM((frames, width, channels), bf16)
    scratch = [
        pltpu.VMEM((2 * frames, 128), f32),
        pltpu.VMEM((tiles - 1, 2 * frames, 128), f32),
        halo,
        halo,
        pltpu.VMEM((frames, cells, channels), bf16),
        pltpu.VMEM((rows, 9 * channels), bf16),
        pltpu.VMEM((rows, 3 * channels), bf16),
        pltpu.VMEM((rows, 3 * channels), bf16),
        dma((tiles - 1,)),
        dma((tiles - 1,)),
        dma((2,)),
        dma((2,)),
        dma((tiles - 1,)),
        dma((tiles - 1,)),
        dma((tiles - 1,)),
        dma((tiles - 1,)),
        dma((copies,)),
        dma((copies,)),
        pltpu.VMEM(video.shape, bf16),
        pltpu.VMEM(gain.shape, f32),
        pltpu.VMEM(bias.shape, f32),
        pltpu.VMEM(sw.shape, bf16),
        pltpu.VMEM(tw.shape, bf16),
        dma((6,)),
    ]
    return pl.pallas_call(
        functools.partial(block_kernel, dps, tiles, width),
        out_shape=[
            jax.ShapeDtypeStruct((frames // tiles, cells * tiles, channels), bf16),
            jax.ShapeDtypeStruct((chunks, pieces, depth, channels), bf16),
        ],
        in_specs=[pl.BlockSpec(memory_space=pltpu.SMEM)]
        + [pl.BlockSpec(memory_space=pl.ANY)] * 7,
        out_specs=[vmem] * 2,
        scratch_shapes=scratch + bufs,
        compiler_params=pltpu.CompilerParams(
            collective_id=0, has_side_effects=True, vmem_limit_bytes=48 << 20
        ),
    )(lengths, video, strips, cot, gain, bias, sw, tw)


def on_device(
    video_in, clip_lengths, norm_gain, norm_bias, spatial_weight, temporal_weight, cotangent
):
    dps, tiles = lax.axis_size("dp"), lax.axis_size("tile")
    _, frames, strip, width, channels = video_in.shape
    height = strip * tiles
    frame_dev = frames // tiles
    out, total = residual_block(
        clip_lengths,
        video_in[0].reshape(frames, strip * width, channels),
        video_in[0],
        cotangent[0].reshape(frame_dev, height * width, channels),
        norm_gain[None],
        norm_bias[None],
        spatial_weight.reshape(9 * channels, channels),
        temporal_weight.reshape(3 * channels, channels),
        dps,
        tiles,
        6,
    )
    scale = 1.0 / math.sqrt(dps * frames * height * width)
    total = total.reshape(12 * channels, channels)
    spatial, temporal = lax.optimization_barrier(
        (total[: 9 * channels], total[9 * channels :])
    )
    return (
        out.reshape(1, frame_dev, height, width, channels),
        (spatial.astype(jnp.float32) * scale).reshape(3, 3, channels, channels),
        (temporal.astype(jnp.float32) * scale).reshape(3, channels, channels),
    )


def solution(mesh):
    return jax.shard_map(
        on_device,
        mesh=mesh,
        in_specs=(
            P("dp", None, "tile", None, None),
            P("dp", None),
            P(),
            P(),
            P(),
            P(),
            P("dp", "tile", None, None, None),
        ),
        out_specs=(P("dp", "tile", None, None, None), P(), P()),
        check_vma=False,
    )
```
